512 devices in a mesh: grp: 16 (over y_hi, x), seq: 32 (over y_lo, z, core).
Axes of the slice: x: 4, y: 8 (y_hi: 4, y_lo: 2; y = y_hi * 2 + y_lo), z: 8, core: 2. Of those that a mesh axis runs over, the one named last changes fastest.
Arguments:
- giant_q: bfloat16 [16, 4096, 2048], P('grp', 'seq'), may hold values from -192 to 192
- giant_k: bfloat16 [16, 4096, 2048], P('grp', 'seq'), may hold values from -6 to 6
- giant_v: bfloat16 [16, 4096, 2048], P('grp', 'seq'), may hold values from -6 to 6
- giant_len: int32 [16], replicated, may hold values from 2048 to 4096, as said below
- short_q: bfloat16 [16, 32, 128, 2048], P('grp', 'seq'), may hold values from -6 to 6
- short_k: bfloat16 [16, 32, 128, 2048], P('grp', 'seq'), may hold values from -6 to 6
- short_v: bfloat16 [16, 32, 128, 2048], P('grp', 'seq'), may hold values from -6 to 6
- short_len: int32 [16, 32], replicated, may hold values from 32 to 128, as said below
- short_move: int32 [16, 32], replicated, may hold values from 0 to 1
Outputs:
- giant_out: bfloat16 [16, 4096, 2048], P('grp', 'seq')
- short_out: bfloat16 [16, 32, 2, 128, 2048], P('grp', 'seq')
The draws below stay inside these ranges and needn't reach their ends.
Inputs may be any that keep to these rules, and one draw needn't show every extreme that they name: `giant_len`: residues of group g's giant protein; positions at or past it are padding; some group's protein fills all 4096 positions. `short_len`: residues of the short protein at [g, s]; slots at or past it are padding; some protein fills all 128 slots.
All inputs are finite; a program needn't handle non-finite values.
Results may differ from the reference program's by a relative error of at most 0.0068.
Values may be sent and summed in bfloat16 or wider, within the bound.
A program may use at most 64 MiB of HBM per device.

```python
import math
import jax
import jax.numpy as jnp
from jax import lax

HD = 64
HEADS = 32
CAPR = 128
FEATURES = 2048
NTOK = 4096
N_GRP = 16
N_SEQ = 32


def shared_keys(key):
    return jnp.clip(jax.random.normal(key, (N_GRP, NTOK, HEADS * HD), jnp.float32), -6.0, 6.0)


def draw_giant_k(key, part):
    return shared_keys(key).astype(jnp.bfloat16)


def draw_giant_q(key, part):
    common = shared_keys(key)
    key = jax.random.fold_in(key, 11)
    queries = jnp.clip(jax.random.normal(key, common.shape, jnp.float32), -6.0, 6.0)
    return queries.astype(jnp.bfloat16)


def draw_giant_len(key, part):
    key = jax.random.fold_in(key, 23)
    first_key, second_key = jax.random.split(key)
    lengths = jax.random.randint(first_key, (N_GRP,), NTOK // 2, NTOK + 1)
    chosen = jax.random.randint(second_key, (), 0, N_GRP)
    return jnp.where(jnp.arange(N_GRP) == chosen, NTOK, lengths).astype(jnp.int32)


def draw_short_len(key, part):
    key = jax.random.fold_in(key, 37)
    key_one, key_two = jax.random.split(key)
    flat = jax.random.randint(key_one, (N_GRP * N_SEQ,), CAPR // 4, CAPR + 1)
    chosen = jax.random.randint(key_two, (), 0, N_GRP * N_SEQ)
    flat = jnp.where(jnp.arange(N_GRP * N_SEQ) == chosen, CAPR, flat)
    return flat.reshape(N_GRP, N_SEQ).astype(jnp.int32)


def with_ends(entries, key, least, high):
    longest = entries.shape.index(max(entries.shape))
    spots = []
    for shift in (0, 1):
        where = [jax.random.randint(jax.random.fold_in(key, axis), (), 0, length) for axis, length in enumerate(entries.shape)]
        where[longest] = (where[longest] + shift) % entries.shape[longest]
        spots.append(tuple(where))
    return entries.at[spots[0]].set(least).at[spots[1]].set(high)


def level_of(rng, dims, cuts, least, top_value):
    def one(position, parts):
        draws = jax.random.uniform(jax.random.fold_in(jax.random.fold_in(rng, 6), position), (parts,), jnp.float32, least / len(cuts), top_value / len(cuts))
        return jnp.repeat(jnp.exp(draws), dims[position] // parts).reshape((-1,) + (1,) * (len(dims) - position - 1))

    loudness = one(*cuts[0])
    for cut in cuts[1:]:
        loudness = loudness * one(*cut)
    return loudness


def scatter_about(own_key, shape, scale, bound, shards=(), kind=jnp.bfloat16):
    values = jax.random.normal(own_key, shape, jnp.float32) * scale
    if len(shards) > 0:
        values = level_of(own_key, shape, shards, -0.22, 0.18) * values
    return jnp.clip(values, min=-bound, max=bound).astype(kind)


def setup_inputs(seed: int = 0) -> dict:
    splits = jax.random.split(jax.random.key(seed), 10)
    giant_q = draw_giant_q(jax.random.fold_in(splits[9], 71), 0)
    giant_k = draw_giant_k(jax.random.fold_in(splits[9], 71), 0)
    giant_v = scatter_about(splits[2], (N_GRP, NTOK, FEATURES), 1.0, 6.0, ((0, 16), (1, 32)))
    giant_len = draw_giant_len(jax.random.fold_in(splits[9], 71), 0)
    short_q = scatter_about(splits[4], (N_GRP, N_SEQ, CAPR, FEATURES), 1.0, 6.0, ((0, 16), (1, 32)))
    short_k = scatter_about(splits[5], (N_GRP, N_SEQ, CAPR, FEATURES), 1.0, 6.0, ((0, 16), (1, 32)))
    short_v = scatter_about(splits[6], (N_GRP, N_SEQ, CAPR, FEATURES), 1.0, 6.0, ((0, 16), (1, 32)))
    short_len = draw_short_len(jax.random.fold_in(splits[9], 71), 0)
    short_move = with_ends(jax.random.randint(splits[8], (N_GRP, N_SEQ), 0, 2), jax.random.fold_in(splits[8], 1), 0, 1).astype(jnp.int32)
    return dict(giant_q=giant_q, giant_k=giant_k, giant_v=giant_v, giant_len=giant_len, short_q=short_q, short_k=short_k, short_v=short_v, short_len=short_len, short_move=short_move)


rotary_base = 10000.0

def rotary(values_in, places):
    half_dim = values_in.shape[-1] // 2
    frequency = rotary_base ** (-(jnp.arange(half_dim, dtype=jnp.float32) * 2.0) / values_in.shape[-1])
    angles = places[:, None] * frequency[None, :]
    cosine = jnp.concatenate([jnp.cos(angles), jnp.cos(angles)], -1)[:, None, :]
    sine_part = jnp.concatenate([jnp.sin(angles), jnp.sin(angles)], -1)[:, None, :]
    turned = jnp.concatenate([-values_in[..., half_dim:], values_in[..., :half_dim]], -1)
    return values_in * cosine + turned * sine_part

def attend(query_rows, key_rows, value_rows, live_keys):

    def one_head(bundle):
        query_head, key_head, value_head = bundle
        scores = jnp.dot(query_head.astype(jnp.float32), jnp.transpose(key_head.astype(jnp.float32))) / math.sqrt(HD)
        scores = jnp.where(live_keys[None, :], scores, -1e+30)
        running_max = lax.optimization_barrier(jnp.max(scores, -1, keepdims=True))
        weights = jnp.where(live_keys[None, :], jnp.exp(scores - running_max), 0.0)
        weight_sum = lax.optimization_barrier(jnp.sum(weights, -1))
        rounded = lax.optimization_barrier(weights.astype(jnp.bfloat16)).astype(jnp.float32)
        attended = jnp.dot(rounded, value_head.astype(jnp.float32))
        return attended / weight_sum[:, None]
    stacked = (jnp.transpose(query_rows, (1, 0, 2)), jnp.transpose(key_rows, (1, 0, 2)), jnp.transpose(value_rows, (1, 0, 2)))
    return jnp.transpose(lax.map(one_head, stacked), (1, 0, 2))

def one_protein(query_in, key_in, value_in, protein_len, slot_total):
    places = jnp.arange(slot_total, dtype=jnp.int32)
    place_float = places.astype(jnp.float32)
    query_rows = rotary(query_in.astype(jnp.float32).reshape(slot_total, HEADS, HD), place_float).astype(jnp.bfloat16)
    key_rows = rotary(key_in.astype(jnp.float32).reshape(slot_total, HEADS, HD), place_float).astype(jnp.bfloat16)
    live_keys = places < protein_len
    attended = attend(query_rows, key_rows, value_in.reshape(slot_total, HEADS, HD), live_keys)
    attended = jnp.where(live_keys[:, None, None], attended, 0.0)
    return attended.reshape(slot_total, HEADS * HD).astype(jnp.bfloat16)

def reference(giant_q, giant_k, giant_v, giant_len, short_q, short_k, short_v, short_len, short_move):

    def giant_one(bundle):
        return one_protein(bundle[0], bundle[1], bundle[2], bundle[3], NTOK)
    giant_out = lax.map(giant_one, (giant_q, giant_k, giant_v, giant_len))

    def short_one(bundle):
        return one_protein(bundle[0], bundle[1], bundle[2], bundle[3], CAPR)
    flat_count = N_GRP * N_SEQ
    results = lax.map(short_one, (short_q.reshape(flat_count, CAPR, HEADS * HD), short_k.reshape(flat_count, CAPR, HEADS * HD), short_v.reshape(flat_count, CAPR, HEADS * HD), short_len.reshape(flat_count)))
    results = results.reshape(N_GRP, N_SEQ, CAPR, HEADS * HD)
    zeros = jnp.zeros_like(results)
    staying = jnp.where((short_move == 0)[:, :, None, None], results, zeros)
    leaving = jnp.where((short_move == 1)[:, :, None, None], results, zeros)
    incoming = jnp.roll(leaving, 1, axis=0)
    short_out = jnp.stack([staying, incoming], 2)
    return (giant_out, short_out)
```

```python
import functools
import math

import jax
import jax.numpy as jnp
import numpy as np
from jax import lax
from jax.experimental import pallas as pl
from jax.experimental.pallas import tpu as pltpu
from jax.sharding import PartitionSpec as P

HD = 64
HEADS = 32
TOK = 128
FEAT = HEADS * HD
LANES = 128
PAIRS = FEAT // LANES
NY, NZ, NC = 2, 8, 2
SEQ = NY * NZ * NC
NTOK = SEQ * TOK
PER = NY * NC
CHUNK = PER * TOK
HALF = NTOK // 2
LOW = -1e30
MESH = pl.DeviceIdType.MESH
f32 = jnp.float32
bf16 = jnp.bfloat16


def angle_table():
    half = HD // 2
    frequency = np.power(10000.0, -(np.arange(half, dtype=np.float64) * 2.0) / HD)
    places = np.arange(NTOK, dtype=np.float32)
    angles = (places[:, None] * frequency.astype(np.float32)[None, :]).astype(np.float64)
    cosine, sine = np.cos(angles), np.sin(angles)
    return np.concatenate([cosine, cosine, -sine, sine], -1).astype(np.float32)


def offset(step):
    return ((step + 1) // 2) * (2 * (step % 2) - 1)


def lanes(rows):
    return lax.broadcasted_iota(jnp.int32, (rows, LANES), 1)


def turn_matrix():
    row = lax.broadcasted_iota(jnp.int32, (LANES, LANES), 0)
    col = lax.broadcasted_iota(jnp.int32, (LANES, LANES), 1)
    partner = jnp.where(col % HD < HD // 2, col + HD // 2, col - HD // 2)
    return jnp.where(row == partner, 1.0, 0.0).astype(bf16)


def swap(x):
    return pltpu.roll(x, HD, 1)


def main_kernel(
    glen, slen, smove, table, gq, gk, gv, sq, sk, sv,
    o_recv, stay_out, in_out,
    xin, tab, cosine, sine, qpack, kvpack, qin, kvin, qaug, acc, top, opack, stay, leave,
    in_sem, tab_sem, own_sem, q_ss, q_rs, kv_ss, kv_rs, o_ss, o_rs, move_sem,
):
    me = lax.axis_index("seq")
    grp = lax.axis_index("grp")
    groups = lax.axis_size("grp")
    core, zed, why = me % NC, (me // NC) % NZ, me // (NC * NZ)
    mine = why * NC + core

    def seq_at(i, z):
        return ((i // NC) * NZ + (z + NZ) % NZ) * NC + i % NC

    def target(step, i):
        return seq_at(i, zed - offset(step))

    def source(step, i):
        return seq_at(i, zed + offset(step))

    def dev(seq):
        return {"grp": grp, "seq": seq}

    def other(t):
        return (mine + t) % PER

    loads = [
        pltpu.make_async_copy(ref.at[0] if n < 3 else ref.at[0, 0], xin.at[n], in_sem.at[n])
        for n, ref in enumerate((gq, gk, gv, sq, sk, sv))
    ]
    own_rows = pl.ds(pl.multiple_of(me * TOK, TOK), TOK)
    tabs = [
        pltpu.make_async_copy(table.at[own_rows], tab.at[0], tab_sem.at[0]),
        pltpu.make_async_copy(table.at[pl.ds(0, TOK)], tab.at[1], tab_sem.at[1]),
    ]
    tabs[0].start()
    for load in loads:
        load.start()
    tabs[1].start()

    barrier = pltpu.get_barrier_semaphore()
    after = {"grp": (grp + 1) % groups, "seq": me}
    before = {"grp": (grp + groups - 1) % groups, "seq": me}

    def greet(t, _):
        pl.semaphore_signal(barrier, 1, device_id=dev((me + t) % SEQ), device_id_type=MESH)
        return 0

    lax.fori_loop(1, SEQ, greet, 0)
    pl.semaphore_signal(barrier, 1, device_id=before, device_id_type=MESH)

    turn = turn_matrix()
    low_half = lanes(TOK) < HD
    low_64 = lanes(HD) < HD

    def spread(n):
        t = tab[n]
        swapped = swap(t)
        cosine[...] = jnp.where(low_half, t, swapped)
        sine[...] = jnp.where(low_half, swapped, t)

    def rotated(x):
        turned = jnp.dot(x, turn, preferred_element_type=f32)
        return x.astype(f32) * cosine[...] + turned * sine[...]

    def cols(j):
        return pl.ds(pl.multiple_of(j * LANES, LANES), LANES)

    tabs[0].wait()
    spread(0)
    loads[0].wait()

    def pack_q(n, _):
        for u in range(4):
            j = n * 4 + u
            x = rotated(xin[0, :, cols(j)]) * (1.0 / math.sqrt(HD))
            upper, lower = x[:HD], x[HD:]
            qpack[2 * j] = jnp.where(low_64, upper, swap(lower)).astype(bf16)
            qpack[2 * j + 1] = jnp.where(low_64, swap(upper), lower).astype(bf16)
        return 0

    lax.fori_loop(0, PAIRS // 4, pack_q, 0)
    pl.semaphore_wait(barrier, SEQ)

    def q_copy(step, i, slot):
        to = target(step, i)
        return pltpu.make_async_remote_copy(
            qpack.at[to], qin.at[step, slot], q_ss.at[step, i], q_rs.at[step, slot],
            device_id=dev(to), device_id_type=MESH,
        )

    def kv_copy(step, i, slot):
        to = target(step, i)
        rows = pl.ds(pl.multiple_of(slot * TOK, TOK), TOK)
        return pltpu.make_async_remote_copy(
            kvpack.at[to], kvin.at[step, rows], kv_ss.at[step, i], kv_rs.at[step, slot],
            device_id=dev(to), device_id_type=MESH,
        )

    def o_copy(step, i):
        to = source(step, i)
        return pltpu.make_async_remote_copy(
            opack.at[step, i], o_recv.at[me], o_ss.at[step, i], o_rs.at[me],
            device_id=dev(to), device_id_type=MESH,
        )

    def send_all(copy):
        for t in range(1, PER):
            copy(0, other(t), mine).start()

        def pair(n, _):
            for i in range(PER):
                copy(2 * n + 1, i, mine).start()
                copy(2 * n + 2, i, mine).start()
            return 0

        lax.fori_loop(0, NZ // 2 - 1, pair, 0)
        for i in range(PER):
            copy(NZ - 1, i, mine).start()

    own_q = pltpu.make_async_copy(qpack.at[me], qin.at[0, mine], own_sem.at[0])
    own_kv = pltpu.make_async_copy(
        kvpack.at[me], kvin.at[0, pl.ds(pl.multiple_of(mine * TOK, TOK), TOK)], own_sem.at[1]
    )
    send_all(q_copy)
    own_q.start()

    loads[1].wait()
    loads[2].wait()

    def pack_kv(n, _):
        for u in range(4):
            j = n * 4 + u
            k = rotated(xin[1, :, cols(j)])
            v = xin[2, :, cols(j)].astype(f32)
            kvpack[2 * j] = jnp.where(low_half, k, swap(v)).astype(bf16)
            kvpack[2 * j + 1] = jnp.where(low_half, swap(k), v).astype(bf16)
        return 0

    lax.fori_loop(0, PAIRS // 4, pack_kv, 0)
    send_all(kv_copy)
    own_kv.start()

    own_len = slen[grp, me]
    own_move = smove[grp, me]
    tabs[1].wait()
    spread(1)
    for n in (3, 4, 5):
        loads[n].wait()
    slot_row = lax.broadcasted_iota(jnp.int32, (TOK, LANES), 0)
    key_live = lax.broadcasted_iota(jnp.int32, (2 * TOK, LANES), 1) < own_len
    row_live = slot_row < own_len

    def short_pair(n, _):
        for u in range(4):
            j = n * 4 + u
            q = rotated(xin[3, :, cols(j)]) * (1.0 / math.sqrt(HD))
            k = rotated(xin[4, :, cols(j)]).astype(bf16)
            stacked = jnp.concatenate([jnp.where(low_half, q, 0.0), jnp.where(low_half, 0.0, q)], 0)
            s = lax.dot_general(
                stacked.astype(bf16), k, (((1,), (1,)), ((), ())), preferred_element_type=f32
            )
            s = jnp.where(key_live, s, LOW)
            p = jnp.exp(s - jnp.max(s, axis=1, keepdims=True))
            p = jnp.where(key_live, p, 0.0).astype(bf16)
            total = jnp.dot(p, jnp.ones((TOK, LANES), bf16), preferred_element_type=f32)
            a = jnp.dot(p, xin[5, :, cols(j)], preferred_element_type=f32) / total
            result = jnp.where(row_live, jnp.where(low_half, a[:TOK], a[TOK:]), 0.0)
            stay[:, cols(j)] = jnp.where(own_move == 0, result, 0.0).astype(bf16)
            leave[:, cols(j)] = jnp.where(own_move == 1, result, 0.0).astype(bf16)
        return 0

    lax.fori_loop(0, PAIRS // 4, short_pair, 0)
    move_copy = pltpu.make_async_remote_copy(
        leave, in_out, move_sem.at[0], move_sem.at[1], device_id=after, device_id_type=MESH
    )
    move_copy.start()
    stay_copy = pltpu.make_async_copy(stay, stay_out, own_sem.at[2])
    stay_copy.start()

    acc[...] = jnp.zeros_like(acc)
    top[...] = jnp.full_like(top, LOW)
    one_lane = jnp.where(lanes(HD) == HD, 1.0, 0.0)

    def open_q(step, i):
        x = qin[step, i].astype(f32)
        rows = pl.multiple_of((step * PER + i) * TOK, TOK)
        qaug[pl.ds(rows, HD)] = jnp.where(low_64, x, one_lane).astype(bf16)
        qaug[pl.ds(rows + HD, HD)] = jnp.where(low_64, swap(x), one_lane).astype(bf16)

    def take_first(copy, own):
        own.wait()
        for t in range(1, PER):
            copy(0, other(t), other(t)).wait_recv()

    take_first(q_copy, own_q)
    for i in range(PER):
        open_q(0, i)

    def open_step(step, _):
        for i in range(PER):
            q_copy(step, i, i).wait_recv()
            open_q(step, i)
        return 0

    lax.fori_loop(1, NZ, open_step, 0)

    group_len = glen[grp]
    chunk_lane = lanes(CHUNK)
    chunk_row = lax.broadcasted_iota(jnp.int32, (CHUNK, LANES), 0)
    half_chunk = NC * TOK

    def operands(step):
        kv = kvin[step]
        zsrc = (zed + offset(step) + NZ) % NZ
        place = (
            (chunk_row // half_chunk) * (NZ * half_chunk) + zsrc * half_chunk + chunk_row % half_chunk
        )
        dead = jnp.where((chunk_lane == HD) & (place >= group_len), LOW, 0.0).astype(bf16)
        keys = jnp.where(chunk_lane < HD, kv, dead)
        values = jnp.where(chunk_lane < HD, jnp.ones((), bf16), kv)
        return keys, values

    def attend(keys, values, rows):
        s = lax.dot_general(
            qaug[rows], keys, (((1,), (1,)), ((), ())), preferred_element_type=f32
        )
        old = top[rows]
        new = jnp.maximum(old, jnp.max(s, axis=1, keepdims=True))
        p = jnp.exp(s - jnp.concatenate([new] * (CHUNK // LANES), 1))
        top[rows] = new
        acc[rows] = acc[rows] * jnp.exp(old - new) + jnp.dot(
            p.astype(bf16), values, preferred_element_type=f32
        )

    def whole_step(step):
        keys, values = operands(step)
        for half in range(2):
            attend(keys, values, pl.ds(half * HALF, HALF))

    take_first(kv_copy, own_kv)

    def one_step(step, _):
        @pl.when(step > 0)
        def _():
            for i in range(PER):
                kv_copy(step, i, i).wait_recv()

        whole_step(step)
        return 0

    lax.fori_loop(0, NZ - 1, one_step, 0)

    last = NZ - 1
    for i in range(PER):
        kv_copy(last, i, i).wait_recv()
    keys, values = operands(last)

    def close(step, i):
        rows = pl.multiple_of((step * PER + i) * TOK, TOK)
        upper, lower = acc[pl.ds(rows, HD)], acc[pl.ds(rows + HD, HD)]
        opack[step, i] = jnp.where(
            low_64, swap(upper) / upper, lower / swap(lower)
        ).astype(bf16)

    def close_step(n, high):
        step = high - n
        for i in range(PER):
            close(step, i)
            o_copy(step, i).start()
        return 0

    attend(keys, values, pl.ds(HALF, HALF))
    lax.fori_loop(0, NZ // 2, lambda n, _: close_step(n, NZ - 1), 0)
    attend(keys, values, pl.ds(0, HALF))
    lax.fori_loop(0, NZ // 2 - 1, lambda n, _: close_step(n, NZ // 2 - 1), 0)
    for t in range(1, PER):
        close(0, other(t))
        o_copy(0, other(t)).start()
    close(0, mine)
    own_o = pltpu.make_async_copy(opack.at[0, mine], o_recv.at[me], own_sem.at[3])
    own_o.start()

    for t in range(1, PER):
        q_copy(0, other(t), mine).wait_send()
        kv_copy(0, other(t), mine).wait_send()
        o_copy(0, other(t)).wait_send()

    def sent(step, _):
        for i in range(PER):
            q_copy(step, i, mine).wait_send()
            kv_copy(step, i, mine).wait_send()
            o_copy(step, i).wait_send()
        return 0

    lax.fori_loop(1, NZ, sent, 0)

    def arrived(t, _):
        head = (me + t) % SEQ
        pltpu.make_async_remote_copy(
            opack.at[0, 0], o_recv.at[head], o_ss.at[0, 0], o_rs.at[head],
            device_id=dev(head), device_id_type=MESH,
        ).wait_recv()
        return 0

    lax.fori_loop(1, SEQ, arrived, 0)
    move_copy.wait()
    stay_copy.wait()
    own_o.wait()


def unpack_kernel(glen, heads, stay, incoming, giant_out, short_out):
    me = lax.axis_index("seq")
    group_len = glen[lax.axis_index("grp")]
    low = lanes(HD) < HD
    row = me * TOK + lax.broadcasted_iota(jnp.int32, (HD, LANES), 0)
    for j in range(PAIRS):
        even, odd = heads[2 * j].astype(f32), heads[2 * j + 1].astype(f32)
        upper = jnp.where(low, even, swap(odd))
        lower = jnp.where(low, swap(even), odd)
        at = pl.ds(j * LANES, LANES)
        giant_out[0, pl.ds(0, HD), at] = jnp.where(row < group_len, upper, 0.0).astype(bf16)
        giant_out[0, pl.ds(HD, HD), at] = jnp.where(row + HD < group_len, lower, 0.0).astype(bf16)
    short_out[0, 0, 0] = stay[...]
    short_out[0, 0, 1] = incoming[...]


def per_device(table, giant_q, giant_k, giant_v, giant_len, short_q, short_k, short_v, short_len, short_move):
    any_spec = pl.BlockSpec(memory_space=pl.ANY)
    smem = pl.BlockSpec(memory_space=pltpu.SMEM)
    vmem = pl.BlockSpec(memory_space=pltpu.VMEM)
    dma = pltpu.SemaphoreType.DMA
    heads, stay, incoming = pl.pallas_call(
        main_kernel,
        out_shape=(
            jax.ShapeDtypeStruct((HEADS, HD, LANES), bf16),
            jax.ShapeDtypeStruct((TOK, FEAT), bf16),
            jax.ShapeDtypeStruct((TOK, FEAT), bf16),
        ),
        in_specs=[smem] * 3 + [any_spec] * 7,
        out_specs=(any_spec,) * 3,
        scratch_shapes=[
            pltpu.VMEM((6, TOK, FEAT), bf16),
            pltpu.VMEM((2, TOK, LANES), f32),
            pltpu.VMEM((TOK, LANES), f32),
            pltpu.VMEM((TOK, LANES), f32),
            pltpu.VMEM((SEQ, HD, LANES), bf16),
            pltpu.VMEM((SEQ, TOK, LANES), bf16),
            pltpu.VMEM((NZ, PER, HD, LANES), bf16),
            pltpu.VMEM((NZ, CHUNK, LANES), bf16),
            pltpu.VMEM((NTOK, LANES), bf16),
            pltpu.VMEM((NTOK, LANES), f32),
            pltpu.VMEM((NTOK, LANES), f32),
            pltpu.VMEM((NZ, PER, HD, LANES), bf16),
            pltpu.VMEM((TOK, FEAT), bf16),
            pltpu.VMEM((TOK, FEAT), bf16),
            dma((6,)),
            dma((2,)),
            dma((4,)),
            dma((NZ, PER)),
            dma((NZ, PER)),
            dma((NZ, PER)),
            dma((NZ, PER)),
            dma((NZ, PER)),
            dma((SEQ,)),
            dma((2,)),
        ],
        compiler_params=pltpu.CompilerParams(
            collective_id=0, has_side_effects=True, vmem_limit_bytes=56 << 20
        ),
    )(giant_len, short_len, short_move, table, giant_q, giant_k, giant_v, short_q, short_k, short_v)
    return pl.pallas_call(
        unpack_kernel,
        out_shape=(
            jax.ShapeDtypeStruct((1, TOK, FEAT), bf16),
            jax.ShapeDtypeStruct((1, 1, 2, TOK, FEAT), bf16),
        ),
        in_specs=[smem] + [vmem] * 3,
        out_specs=(vmem, vmem),
        compiler_params=pltpu.CompilerParams(vmem_limit_bytes=32 << 20),
    )(giant_len, heads, stay, incoming)


def solution(mesh):
    table = angle_table()
    in_specs = (
        P(),
        P("grp", "seq", None),
        P("grp", "seq", None),
        P("grp", "seq", None),
        P(),
        P("grp", "seq", None, None),
        P("grp", "seq", None, None),
        P("grp", "seq", None, None),
        P(),
        P(),
    )
    out_specs = (P("grp", "seq", None), P("grp", "seq", None, None, None))
    body = jax.shard_map(
        per_device, mesh=mesh, in_specs=in_specs, out_specs=out_specs, check_vma=False
    )

    def run(*arrays):
        return body(jnp.asarray(table), *arrays)

    return run
```

```python
import functools
import math

import jax
import jax.numpy as jnp
import numpy as np
from jax import lax
from jax.experimental import pallas as pl
from jax.experimental.pallas import tpu as pltpu
from jax.sharding import PartitionSpec as P

HD = 64
HEADS = 32
TOK = 128
FEAT = HEADS * HD
LANES = 128
PAIRS = FEAT // LANES
NY, NZ, NC = 2, 8, 2
SEQ = NY * NZ * NC
NTOK = SEQ * TOK
PER = NY * NC
CHUNK = PER * TOK
HALF = NTOK // 2
HALF_BITS = (NC * TOK).bit_length() - 1
EARLY = 4
ROWS = 2 * CHUNK
LOW = -1e30
MESH = pl.DeviceIdType.MESH
f32 = jnp.float32
bf16 = jnp.bfloat16


def angle_table():
    half = HD // 2
    frequency = np.power(10000.0, -(np.arange(half, dtype=np.float64) * 2.0) / HD)
    places = np.arange(NTOK, dtype=np.float32)
    angles = (places[:, None] * frequency.astype(np.float32)[None, :]).astype(np.float64)
    cosine, sine = np.cos(angles), np.sin(angles)
    return np.concatenate([cosine, cosine, -sine, sine], -1).astype(np.float32)


def offset(step):
    return ((step + 1) // 2) * (2 * (step % 2) - 1)


def lanes(rows):
    return lax.broadcasted_iota(jnp.int32, (rows, LANES), 1)


def turn_matrix():
    row = lax.broadcasted_iota(jnp.int32, (LANES, LANES), 0)
    col = lax.broadcasted_iota(jnp.int32, (LANES, LANES), 1)
    partner = jnp.where(col % HD < HD // 2, col + HD // 2, col - HD // 2)
    return jnp.where(row == partner, 1.0, 0.0).astype(bf16)


def swap(x):
    return pltpu.roll(x, HD, 1)


def main_kernel(
    glen, slen, smove, table, gq, gk, gv, sq, sk, sv,
    o_recv, stay_out, in_out,
    xin, tab, cosine, sine, qpack, kvpack, qin, kvin, qaug, acc, top, late_k, late_v, opack, stay, leave,
    in_sem, tab_sem, own_sem, q_ss, q_rs, kv_ss, kv_rs, o_ss, o_rs, move_ss, move_rs,
):
    me = lax.axis_index("seq")
    grp = lax.axis_index("grp")
    groups = lax.axis_size("grp")
    core, zed, why = me % NC, (me // NC) % NZ, me // (NC * NZ)
    mine = why * NC + core

    def seq_at(i, z):
        return ((i // NC) * NZ + (z + NZ) % NZ) * NC + i % NC

    def target(step, i):
        return seq_at(i, zed - offset(step))

    def source(step, i):
        return seq_at(i, zed + offset(step))

    def dev(seq):
        return {"grp": grp, "seq": seq}

    def other(t):
        return (mine + t) % PER

    loads = [
        pltpu.make_async_copy(ref.at[0] if n < 3 else ref.at[0, 0], xin.at[n], in_sem.at[n])
        for n, ref in enumerate((gq, gk, gv, sq, sk, sv))
    ]
    own_rows = pl.ds(pl.multiple_of(me * TOK, TOK), TOK)
    tabs = [
        pltpu.make_async_copy(table.at[own_rows], tab.at[0], tab_sem.at[0]),
        pltpu.make_async_copy(table.at[pl.ds(0, TOK)], tab.at[1], tab_sem.at[1]),
    ]
    tabs[0].start()
    for load in loads:
        load.start()
    tabs[1].start()

    barrier = pltpu.get_barrier_semaphore()
    after = {"grp": (grp + 1) % groups, "seq": me}
    before = {"grp": (grp + groups - 1) % groups, "seq": me}

    def greet(t, _):
        pl.semaphore_signal(barrier, 1, device_id=dev((me + t) % SEQ), device_id_type=MESH)
        return 0

    lax.fori_loop(1, SEQ, greet, 0)
    pl.semaphore_signal(barrier, 1, device_id=before, device_id_type=MESH)

    turn = turn_matrix()
    low_half = lanes(TOK) < HD
    low_64 = lanes(HD) < HD

    def spread(n):
        t = tab[n]
        swapped = swap(t)
        cosine[...] = jnp.where(low_half, t, swapped)
        sine[...] = jnp.where(low_half, swapped, t)

    def rotated(x):
        turned = jnp.dot(x, turn, preferred_element_type=f32)
        return x.astype(f32) * cosine[...] + turned * sine[...]

    def cols(j):
        return pl.ds(pl.multiple_of(j * LANES, LANES), LANES)

    tabs[0].wait()
    spread(0)
    loads[0].wait()

    pl.semaphore_wait(barrier, SEQ)

    def q_copy(step, i, slot):
        to = target(step, i)
        return pltpu.make_async_remote_copy(
            qpack.at[to], qin.at[step, slot], q_ss.at[step, i], q_rs.at[step, slot],
            device_id=dev(to), device_id_type=MESH,
        )

    def kv_copy(step, i, slot):
        to = target(step, i)
        rows = pl.ds(pl.multiple_of(slot * TOK, TOK), TOK)
        return pltpu.make_async_remote_copy(
            kvpack.at[to], kvin.at[step, rows], kv_ss.at[step, i], kv_rs.at[step, slot],
            device_id=dev(to), device_id_type=MESH,
        )

    def o_copy(step, i):
        to = source(step, i)
        return pltpu.make_async_remote_copy(
            opack.at[step, i], o_recv.at[me], o_ss.at[step, i], o_rs.at[me],
            device_id=dev(to), device_id_type=MESH,
        )

    def pack_q(step, y):
        j = y * NZ + (zed - offset(step) + NZ) % NZ
        x = rotated(xin[0, :, cols(j)]) * (1.0 / math.sqrt(HD))
        upper, lower = x[:HD], x[HD:]
        qpack[2 * j] = jnp.where(low_64, upper, swap(lower)).astype(bf16)
        qpack[2 * j + 1] = jnp.where(low_64, swap(upper), lower).astype(bf16)

    def send_q(step, _):
        for y in range(NY):
            pack_q(step, y)
            for c in range(NC):
                q_copy(step, y * NC + c, mine).start()
        return 0

    def send_first(copy):
        for t in range(1, PER):
            copy(0, other(t), mine).start()

    own_q = pltpu.make_async_copy(qpack.at[me], qin.at[0, mine], own_sem.at[0])
    own_kv = pltpu.make_async_copy(
        kvpack.at[me], kvin.at[0, pl.ds(pl.multiple_of(mine * TOK, TOK), TOK)], own_sem.at[1]
    )
    for y in range(NY):
        pack_q(0, y)
    send_first(q_copy)
    own_q.start()
    lax.fori_loop(1, NZ, send_q, 0)

    loads[1].wait()
    loads[2].wait()

    def pack_kv(n, _):
        for u in range(4):
            j = n * 4 + u
            k = rotated(xin[1, :, cols(j)])
            v = xin[2, :, cols(j)].astype(f32)
            kvpack[2 * j] = jnp.where(low_half, k, swap(v)).astype(bf16)
            kvpack[2 * j + 1] = jnp.where(low_half, swap(k), v).astype(bf16)
        return 0

    lax.fori_loop(0, PAIRS // 4, pack_kv, 0)
    own_len = slen[grp, me]
    own_move = smove[grp, me]
    tabs[1].wait()
    spread(1)
    for n in (3, 4, 5):
        loads[n].wait()
    slot_row = lax.broadcasted_iota(jnp.int32, (TOK, LANES), 0)
    key_live = lax.broadcasted_iota(jnp.int32, (2 * TOK, LANES), 1) < own_len
    row_live = slot_row < own_len

    def short_pair(n, _):
        for u in range(4):
            j = n * 4 + u
            q = rotated(xin[3, :, cols(j)]) * (1.0 / math.sqrt(HD))
            k = rotated(xin[4, :, cols(j)]).astype(bf16)
            stacked = jnp.concatenate([jnp.where(low_half, q, 0.0), jnp.where(low_half, 0.0, q)], 0)
            s = lax.dot_general(
                stacked.astype(bf16), k, (((1,), (1,)), ((), ())), preferred_element_type=f32
            )
            s = jnp.where(key_live, s, LOW)
            p = jnp.exp(s - jnp.max(s, axis=1, keepdims=True))
            p = jnp.where(key_live, p, 0.0).astype(bf16)
            total = jnp.dot(p, jnp.ones((TOK, LANES), bf16), preferred_element_type=f32)
            a = jnp.dot(p, xin[5, :, cols(j)], preferred_element_type=f32) / total
            result = jnp.where(row_live, jnp.where(low_half, a[:TOK], a[TOK:]), 0.0)
            stay[:, cols(j)] = jnp.where(own_move == 0, result, 0.0).astype(bf16)
            leave[:, cols(j)] = jnp.where(own_move == 1, result, 0.0).astype(bf16)
        return 0

    lax.fori_loop(0, PAIRS // 4, short_pair, 0)
    send_first(kv_copy)
    own_kv.start()

    def send_pair(n, _):
        for i in range(PER):
            kv_copy(2 * n + 1, i, mine).start()
            kv_copy(2 * n + 2, i, mine).start()
        return 0

    lax.fori_loop(0, NZ // 2 - 1, send_pair, 0)
    for i in range(PER):
        kv_copy(NZ - 1, i, mine).start()


    def move_copy(n):
        rows = pl.ds(pl.multiple_of(n * (TOK // NZ), TOK // NZ), TOK // NZ)
        return pltpu.make_async_remote_copy(
            leave.at[rows], in_out.at[rows], move_ss.at[n], move_rs.at[n],
            device_id=after, device_id_type=MESH,
        )

    stay_copy = pltpu.make_async_copy(stay, stay_out, own_sem.at[2])
    stay_copy.start()

    acc[...] = jnp.zeros_like(acc)
    top[...] = jnp.full_like(top, LOW)
    one_lane = jnp.where(lanes(HD) == HD, 1.0, 0.0)

    def open_q(step, i):
        x = qin[step, i].astype(f32)
        rows = pl.multiple_of((step * PER + i) * TOK, TOK)
        qaug[pl.ds(rows, HD)] = jnp.where(low_64, x, one_lane).astype(bf16)
        qaug[pl.ds(rows + HD, HD)] = jnp.where(low_64, swap(x), one_lane).astype(bf16)

    def take_first(copy, own):
        own.wait()
        for t in range(1, PER):
            copy(0, other(t), other(t)).wait_recv()

    def open_step(step, _):
        for i in range(PER):
            q_copy(step, i, i).wait_recv()
            open_q(step, i)
        return 0

    take_first(q_copy, own_q)
    for i in range(PER):
        open_q(0, i)
    lax.fori_loop(1, NZ, open_step, 0)

    group_len = glen[grp]
    chunk_lane = lanes(CHUNK)
    chunk_row = lax.broadcasted_iota(jnp.int32, (CHUNK, LANES), 0)
    half_chunk = NC * TOK

    def operands(step):
        kv = kvin[step]
        zsrc = (zed + offset(step) + NZ) % NZ
        place = (
            (chunk_row >> HALF_BITS) * (NZ * half_chunk)
            + zsrc * half_chunk
            + (chunk_row & (half_chunk - 1))
        )
        dead = jnp.where((chunk_lane == HD) & (place >= group_len), LOW, 0.0).astype(bf16)
        keys = jnp.where(chunk_lane < HD, kv, dead)
        values = jnp.where(chunk_lane < HD, jnp.ones((), bf16), kv)
        return keys, values

    def attend(keys, values, rows):
        s = lax.dot_general(
            qaug[rows], keys, (((1,), (1,)), ((), ())), preferred_element_type=f32
        )
        old = top[rows]
        new = jnp.maximum(old, jnp.max(s, axis=1, keepdims=True))
        p = jnp.exp(s - jnp.concatenate([new] * (keys.shape[0] // LANES), 1))
        top[rows] = new
        acc[rows] = acc[rows] * jnp.exp(old - new) + jnp.dot(
            p.astype(bf16), values, preferred_element_type=f32
        )

    take_first(kv_copy, own_kv)

    def one_step(step, _):
        @pl.when(step > 0)
        def _():
            for i in range(PER):
                kv_copy(step, i, i).wait_recv()

        keys, values = operands(step)
        attend(keys, values, pl.ds(0, HALF))

        move_copy(2 * step).start()
        attend(keys, values, pl.ds(HALF, HALF))
        move_copy(2 * step + 1).start()
        return 0

    lax.fori_loop(0, EARLY, one_step, 0)

    def ready(step, _):
        for i in range(PER):
            kv_copy(step, i, i).wait_recv()
        rows = pl.ds(pl.multiple_of((step - EARLY) * CHUNK, CHUNK), CHUNK)
        late_k[rows], late_v[rows] = operands(step)
        return 0

    lax.fori_loop(EARLY, NZ, ready, 0)

    def rest(group):
        rows = pl.ds(pl.multiple_of(group * ROWS, ROWS), ROWS)
        for n in range((NZ - EARLY) // 2):
            at = pl.ds(n * 2 * CHUNK, 2 * CHUNK)
            attend(late_k[at], late_v[at], rows)

    def close(step, i):
        rows = pl.multiple_of((step * PER + i) * TOK, TOK)
        upper, lower = acc[pl.ds(rows, HD)], acc[pl.ds(rows + HD, HD)]
        opack[step, i] = jnp.where(
            low_64, swap(upper) / upper, lower / swap(lower)
        ).astype(bf16)

    def finish(n, _):
        group = NZ // 2 - 1 - n
        rest(group)
        for step in (2 * group + 1, 2 * group):
            for i in range(PER):
                close(step, i)
                o_copy(step, i).start()
        return 0

    lax.fori_loop(0, NZ // 2 - 1, finish, 0)
    rest(0)
    for i in range(PER):
        close(1, i)
        o_copy(1, i).start()
    for t in range(1, PER):
        close(0, other(t))
        o_copy(0, other(t)).start()
    close(0, mine)
    own_o = pltpu.make_async_copy(opack.at[0, mine], o_recv.at[me], own_sem.at[3])
    own_o.start()

    for t in range(1, PER):
        q_copy(0, other(t), mine).wait_send()
        kv_copy(0, other(t), mine).wait_send()
        o_copy(0, other(t)).wait_send()

    def sent(step, _):
        for i in range(PER):
            q_copy(step, i, mine).wait_send()
            kv_copy(step, i, mine).wait_send()
            o_copy(step, i).wait_send()
        return 0

    lax.fori_loop(1, NZ, sent, 0)

    def arrived(t, _):
        head = (me + t) % SEQ
        pltpu.make_async_remote_copy(
            opack.at[0, 0], o_recv.at[head], o_ss.at[0, 0], o_rs.at[head],
            device_id=dev(head), device_id_type=MESH,
        ).wait_recv()
        return 0

    lax.fori_loop(1, SEQ, arrived, 0)

    def moved(n, _):
        move_copy(n).wait()
        return 0

    lax.fori_loop(0, NZ, moved, 0)
    stay_copy.wait()
    own_o.wait()


PARTS = 4


def unpack_kernel(glen, heads, stay, incoming, giant_out, short_out, held, made, both, sems):
    moves = [
        pltpu.make_async_copy(ref, both.at[n], sems.at[n]) for n, ref in enumerate((stay, incoming))
    ]
    ends = [
        pltpu.make_async_copy(both.at[n], short_out.at[0, 0, n], sems.at[2 + 2 * PARTS + n])
        for n in range(2)
    ]
    per = HEADS // PARTS
    wide = FEAT // PARTS
    into = [
        pltpu.make_async_copy(
            heads.at[pl.ds(n * per, per)], held.at[pl.ds(n * per, per)], sems.at[2 + n]
        )
        for n in range(PARTS)
    ]
    out = [
        pltpu.make_async_copy(
            made.at[:, pl.ds(n * wide, wide)], giant_out.at[0, :, pl.ds(n * wide, wide)],
            sems.at[2 + PARTS + n],
        )
        for n in range(PARTS)
    ]
    for copy in moves + into:
        copy.start()
    for copy, end in zip(moves, ends):
        copy.wait()
        end.start()
    me = lax.axis_index("seq")
    group_len = glen[lax.axis_index("grp")]
    low = lanes(HD) < HD
    row = me * TOK + lax.broadcasted_iota(jnp.int32, (HD, LANES), 0)
    for n in range(PARTS):
        into[n].wait()
        for j in range(n * PAIRS // PARTS, (n + 1) * PAIRS // PARTS):
            even, odd = held[2 * j].astype(f32), held[2 * j + 1].astype(f32)
            upper = jnp.where(low, even, swap(odd))
            lower = jnp.where(low, swap(even), odd)
            at = pl.ds(j * LANES, LANES)
            made[pl.ds(0, HD), at] = jnp.where(row < group_len, upper, 0.0).astype(bf16)
            made[pl.ds(HD, HD), at] = jnp.where(row + HD < group_len, lower, 0.0).astype(bf16)
        out[n].start()
    for copy in out + ends:
        copy.wait()


def per_device(table, giant_q, giant_k, giant_v, giant_len, short_q, short_k, short_v, short_len, short_move):
    any_spec = pl.BlockSpec(memory_space=pl.ANY)
    smem = pl.BlockSpec(memory_space=pltpu.SMEM)
    dma = pltpu.SemaphoreType.DMA
    heads, stay, incoming = pl.pallas_call(
        main_kernel,
        out_shape=(
            jax.ShapeDtypeStruct((HEADS, HD, LANES), bf16),
            jax.ShapeDtypeStruct((TOK, FEAT), bf16),
            jax.ShapeDtypeStruct((TOK, FEAT), bf16),
        ),
        in_specs=[smem] * 3 + [any_spec] * 7,
        out_specs=(any_spec,) * 3,
        scratch_shapes=[
            pltpu.VMEM((6, TOK, FEAT), bf16),
            pltpu.VMEM((2, TOK, LANES), f32),
            pltpu.VMEM((TOK, LANES), f32),
            pltpu.VMEM((TOK, LANES), f32),
            pltpu.VMEM((SEQ, HD, LANES), bf16),
            pltpu.VMEM((SEQ, TOK, LANES), bf16),
            pltpu.VMEM((NZ, PER, HD, LANES), bf16),
            pltpu.VMEM((NZ, CHUNK, LANES), bf16),
            pltpu.VMEM((NTOK, LANES), bf16),
            pltpu.VMEM((NTOK, LANES), f32),
            pltpu.VMEM((NTOK, LANES), f32),
            pltpu.VMEM(((NZ - EARLY) * CHUNK, LANES), bf16),
            pltpu.VMEM(((NZ - EARLY) * CHUNK, LANES), bf16),
            pltpu.VMEM((NZ, PER, HD, LANES), bf16),
            pltpu.VMEM((TOK, FEAT), bf16),
            pltpu.VMEM((TOK, FEAT), bf16),
            dma((6,)),
            dma((2,)),
            dma((4,)),
            dma((NZ, PER)),
            dma((NZ, PER)),
            dma((NZ, PER)),
            dma((NZ, PER)),
            dma((NZ, PER)),
            dma((SEQ,)),
            dma((NZ,)),
            dma((NZ,)),
        ],
        compiler_params=pltpu.CompilerParams(
            collective_id=0, has_side_effects=True, vmem_limit_bytes=56 << 20
        ),
    )(giant_len, short_len, short_move, table, giant_q, giant_k, giant_v, short_q, short_k, short_v)
    return pl.pallas_call(
        unpack_kernel,
        out_shape=(
            jax.ShapeDtypeStruct((1, TOK, FEAT), bf16),
            jax.ShapeDtypeStruct((1, 1, 2, TOK, FEAT), bf16),
        ),
        in_specs=[smem] + [any_spec] * 3,
        out_specs=(any_spec, any_spec),
        scratch_shapes=[
            pltpu.VMEM((HEADS, HD, LANES), bf16),
            pltpu.VMEM((TOK, FEAT), bf16),
            pltpu.VMEM((2, TOK, FEAT), bf16),
            dma((4 + 2 * PARTS,)),
        ],
        compiler_params=pltpu.CompilerParams(vmem_limit_bytes=56 << 20),
    )(giant_len, heads, stay, incoming)


def solution(mesh):
    table = angle_table()
    in_specs = (
        P(),
        P("grp", "seq", None),
        P("grp", "seq", None),
        P("grp", "seq", None),
        P(),
        P("grp", "seq", None, None),
        P("grp", "seq", None, None),
        P("grp", "seq", None, None),
        P(),
        P(),
    )
    out_specs = (P("grp", "seq", None), P("grp", "seq", None, None, None))
    body = jax.shard_map(
        per_device, mesh=mesh, in_specs=in_specs, out_specs=out_specs, check_vma=False
    )

    def run(*arrays):
        return body(jnp.asarray(table), *arrays)

    return run
```

```python
import functools
import math

import jax
import jax.numpy as jnp
import numpy as np
from jax import lax
from jax.experimental import pallas as pl
from jax.experimental.pallas import tpu as pltpu
from jax.sharding import PartitionSpec as P

HD = 64
HEADS = 32
TOK = 128
FEAT = HEADS * HD
LANES = 128
PAIRS = FEAT // LANES
NY, NZ, NC = 2, 8, 2
SEQ = NY * NZ * NC
NTOK = SEQ * TOK
PER = NY * NC
CHUNK = PER * TOK
HALF = NTOK // 2
HALF_BITS = (NC * TOK).bit_length() - 1
EARLY = 6
ROWS = 2 * CHUNK
LOW = -1e30
MESH = pl.DeviceIdType.MESH
f32 = jnp.float32
bf16 = jnp.bfloat16


def angle_table():
    half = HD // 2
    frequency = np.power(10000.0, -(np.arange(half, dtype=np.float64) * 2.0) / HD)
    places = np.arange(NTOK, dtype=np.float32)
    angles = (places[:, None] * frequency.astype(np.float32)[None, :]).astype(np.float64)
    cosine, sine = np.cos(angles), np.sin(angles)
    return np.concatenate([cosine, cosine, -sine, sine], -1).astype(np.float32)


def offset(step):
    return ((step + 1) // 2) * (2 * (step % 2) - 1)


def lanes(rows):
    return lax.broadcasted_iota(jnp.int32, (rows, LANES), 1)


def turn_matrix():
    row = lax.broadcasted_iota(jnp.int32, (LANES, LANES), 0)
    col = lax.broadcasted_iota(jnp.int32, (LANES, LANES), 1)
    partner = jnp.where(col % HD < HD // 2, col + HD // 2, col - HD // 2)
    return jnp.where(row == partner, 1.0, 0.0).astype(bf16)


def swap(x):
    return pltpu.roll(x, HD, 1)


def main_kernel(
    glen, slen, smove, table, gq, gk, gv, sq, sk, sv,
    o_recv, stay_out, in_out,
    xin, tab, cosine, sine, qpack, kvpack, qin, kvin, qaug, acc, top, late_k, late_v, opack, stay, leave,
    in_sem, tab_sem, own_sem, q_ss, q_rs, kv_ss, kv_rs, o_ss, o_rs, move_ss, move_rs,
):
    me = lax.axis_index("seq")
    grp = lax.axis_index("grp")
    groups = lax.axis_size("grp")
    core, zed, why = me % NC, (me // NC) % NZ, me // (NC * NZ)
    mine = why * NC + core

    def seq_at(i, z):
        return ((i // NC) * NZ + (z + NZ) % NZ) * NC + i % NC

    def target(step, i):
        return seq_at(i, zed - offset(step))

    def source(step, i):
        return seq_at(i, zed + offset(step))

    def dev(seq):
        return {"grp": grp, "seq": seq}

    def other(t):
        return (mine + t) % PER

    loads = [
        pltpu.make_async_copy(ref.at[0] if n < 3 else ref.at[0, 0], xin.at[n], in_sem.at[n])
        for n, ref in enumerate((gq, gk, gv, sq, sk, sv))
    ]
    own_rows = pl.ds(pl.multiple_of(me * TOK, TOK), TOK)
    tabs = [
        pltpu.make_async_copy(table.at[own_rows], tab.at[0], tab_sem.at[0]),
        pltpu.make_async_copy(table.at[pl.ds(0, TOK)], tab.at[1], tab_sem.at[1]),
    ]
    tabs[0].start()
    for load in loads:
        load.start()
    tabs[1].start()

    barrier = pltpu.get_barrier_semaphore()
    after = {"grp": (grp + 1) % groups, "seq": me}
    before = {"grp": (grp + groups - 1) % groups, "seq": me}

    def greet(t, _):
        pl.semaphore_signal(barrier, 1, device_id=dev((me + t) % SEQ), device_id_type=MESH)
        return 0

    lax.fori_loop(1, SEQ, greet, 0)
    pl.semaphore_signal(barrier, 1, device_id=before, device_id_type=MESH)

    turn = turn_matrix()
    low_half = lanes(TOK) < HD
    low_64 = lanes(HD) < HD

    def spread(n):
        t = tab[n]
        swapped = swap(t)
        cosine[...] = jnp.where(low_half, t, swapped)
        sine[...] = jnp.where(low_half, swapped, t)

    def rotated(x):
        turned = jnp.dot(x, turn, preferred_element_type=f32)
        return x.astype(f32) * cosine[...] + turned * sine[...]

    def cols(j):
        return pl.ds(pl.multiple_of(j * LANES, LANES), LANES)

    tabs[0].wait()
    spread(0)
    loads[0].wait()

    pl.semaphore_wait(barrier, SEQ)

    def q_copy(step, i, slot):
        to = target(step, i)
        return pltpu.make_async_remote_copy(
            qpack.at[to], qin.at[step, slot], q_ss.at[step, i], q_rs.at[step, slot],
            device_id=dev(to), device_id_type=MESH,
        )

    def kv_copy(step, i, slot):
        to = target(step, i)
        rows = pl.ds(pl.multiple_of(slot * TOK, TOK), TOK)
        return pltpu.make_async_remote_copy(
            kvpack.at[to], kvin.at[step, rows], kv_ss.at[step, i], kv_rs.at[step, slot],
            device_id=dev(to), device_id_type=MESH,
        )

    def o_copy(step, i):
        to = source(step, i)
        return pltpu.make_async_remote_copy(
            opack.at[step, i], o_recv.at[me], o_ss.at[step, i], o_rs.at[me],
            device_id=dev(to), device_id_type=MESH,
        )

    def pack_q(step, y):
        j = y * NZ + (zed - offset(step) + NZ) % NZ
        x = rotated(xin[0, :, cols(j)]) * (1.0 / math.sqrt(HD))
        upper, lower = x[:HD], x[HD:]
        qpack[2 * j] = jnp.where(low_64, upper, swap(lower)).astype(bf16)
        qpack[2 * j + 1] = jnp.where(low_64, swap(upper), lower).astype(bf16)

    def send_q(step, _):
        for y in range(NY):
            pack_q(step, y)
            for c in range(NC):
                q_copy(step, y * NC + c, mine).start()
        return 0

    def send_first(copy):
        for t in range(1, PER):
            copy(0, other(t), mine).start()

    own_q = pltpu.make_async_copy(qpack.at[me], qin.at[0, mine], own_sem.at[0])
    own_kv = pltpu.make_async_copy(
        kvpack.at[me], kvin.at[0, pl.ds(pl.multiple_of(mine * TOK, TOK), TOK)], own_sem.at[1]
    )
    for y in range(NY):
        pack_q(0, y)
    send_first(q_copy)
    own_q.start()
    lax.fori_loop(1, NZ, send_q, 0)

    loads[1].wait()
    loads[2].wait()

    def pack_kv(n, _):
        for u in range(4):
            j = n * 4 + u
            k = rotated(xin[1, :, cols(j)])
            v = xin[2, :, cols(j)].astype(f32)
            kvpack[2 * j] = jnp.where(low_half, k, swap(v)).astype(bf16)
            kvpack[2 * j + 1] = jnp.where(low_half, swap(k), v).astype(bf16)
        return 0

    lax.fori_loop(0, PAIRS // 4, pack_kv, 0)
    own_len = slen[grp, me]
    own_move = smove[grp, me]
    tabs[1].wait()
    spread(1)
    for n in (3, 4, 5):
        loads[n].wait()
    slot_row = lax.broadcasted_iota(jnp.int32, (TOK, LANES), 0)
    key_live = lax.broadcasted_iota(jnp.int32, (2 * TOK, LANES), 1) < own_len
    row_live = slot_row < own_len

    def short_pair(n, _):
        for u in range(4):
            j = n * 4 + u
            q = rotated(xin[3, :, cols(j)]) * (1.0 / math.sqrt(HD))
            k = rotated(xin[4, :, cols(j)]).astype(bf16)
            stacked = jnp.concatenate([jnp.where(low_half, q, 0.0), jnp.where(low_half, 0.0, q)], 0)
            s = lax.dot_general(
                stacked.astype(bf16), k, (((1,), (1,)), ((), ())), preferred_element_type=f32
            )
            s = jnp.where(key_live, s, LOW)
            p = jnp.exp(s - jnp.max(s, axis=1, keepdims=True))
            p = jnp.where(key_live, p, 0.0).astype(bf16)
            total = jnp.dot(p, jnp.ones((TOK, LANES), bf16), preferred_element_type=f32)
            a = jnp.dot(p, xin[5, :, cols(j)], preferred_element_type=f32) / total
            result = jnp.where(row_live, jnp.where(low_half, a[:TOK], a[TOK:]), 0.0)
            stay[:, cols(j)] = jnp.where(own_move == 0, result, 0.0).astype(bf16)
            leave[:, cols(j)] = jnp.where(own_move == 1, result, 0.0).astype(bf16)
        return 0

    lax.fori_loop(0, PAIRS // 4, short_pair, 0)
    send_first(kv_copy)
    own_kv.start()

    def send_pair(n, _):
        for i in range(PER):
            kv_copy(2 * n + 1, i, mine).start()
            kv_copy(2 * n + 2, i, mine).start()
        return 0

    lax.fori_loop(0, NZ // 2 - 1, send_pair, 0)
    for i in range(PER):
        kv_copy(NZ - 1, i, mine).start()


    def move_copy(n):
        rows = pl.ds(pl.multiple_of(n * (TOK // NZ), TOK // NZ), TOK // NZ)
        return pltpu.make_async_remote_copy(
            leave.at[rows], in_out.at[rows], move_ss.at[n], move_rs.at[n],
            device_id=after, device_id_type=MESH,
        )

    stay_copy = pltpu.make_async_copy(stay, stay_out, own_sem.at[2])
    stay_copy.start()

    acc[...] = jnp.zeros_like(acc)
    top[...] = jnp.full_like(top, LOW)
    one_lane = jnp.where(lanes(HD) == HD, 1.0, 0.0)

    def open_q(step, i):
        x = qin[step, i].astype(f32)
        rows = pl.multiple_of((step * PER + i) * TOK, TOK)
        qaug[pl.ds(rows, HD)] = jnp.where(low_64, x, one_lane).astype(bf16)
        qaug[pl.ds(rows + HD, HD)] = jnp.where(low_64, swap(x), one_lane).astype(bf16)

    def take_first(copy, own):
        own.wait()
        for t in range(1, PER):
            copy(0, other(t), other(t)).wait_recv()

    def open_step(step, _):
        for i in range(PER):
            q_copy(step, i, i).wait_recv()
            open_q(step, i)
        return 0

    take_first(q_copy, own_q)
    for i in range(PER):
        open_q(0, i)
    lax.fori_loop(1, NZ, open_step, 0)

    group_len = glen[grp]
    chunk_lane = lanes(CHUNK)
    chunk_row = lax.broadcasted_iota(jnp.int32, (CHUNK, LANES), 0)
    half_chunk = NC * TOK

    def operands(step):
        kv = kvin[step]
        zsrc = (zed + offset(step) + NZ) % NZ
        place = (
            (chunk_row >> HALF_BITS) * (NZ * half_chunk)
            + zsrc * half_chunk
            + (chunk_row & (half_chunk - 1))
        )
        dead = jnp.where((chunk_lane == HD) & (place >= group_len), LOW, 0.0).astype(bf16)
        keys = jnp.where(chunk_lane < HD, kv, dead)
        values = jnp.where(chunk_lane < HD, jnp.ones((), bf16), kv)
        return keys, values

    def attend(keys, values, rows):
        s = lax.dot_general(
            qaug[rows], keys, (((1,), (1,)), ((), ())), preferred_element_type=f32
        )
        old = top[rows]
        new = jnp.maximum(old, jnp.max(s, axis=1, keepdims=True))
        p = jnp.exp(s - jnp.concatenate([new] * (keys.shape[0] // LANES), 1))
        top[rows] = new
        acc[rows] = acc[rows] * jnp.exp(old - new) + jnp.dot(
            p.astype(bf16), values, preferred_element_type=f32
        )

    take_first(kv_copy, own_kv)

    def one_step(step, _):
        @pl.when(step > 0)
        def _():
            for i in range(PER):
                kv_copy(step, i, i).wait_recv()

        keys, values = operands(step)
        attend(keys, values, pl.ds(0, HALF))

        move_copy(step).start()
        attend(keys, values, pl.ds(HALF, HALF))
        return 0

    lax.fori_loop(0, EARLY, one_step, 0)

    def ready(step, _):
        move_copy(step).start()
        for i in range(PER):
            kv_copy(step, i, i).wait_recv()
        rows = pl.ds(pl.multiple_of((step - EARLY) * CHUNK, CHUNK), CHUNK)
        late_k[rows], late_v[rows] = operands(step)
        return 0

    lax.fori_loop(EARLY, NZ, ready, 0)

    def rest(group):
        rows = pl.ds(pl.multiple_of(group * ROWS, ROWS), ROWS)
        for n in range((NZ - EARLY) // 2):
            at = pl.ds(n * 2 * CHUNK, 2 * CHUNK)
            attend(late_k[at], late_v[at], rows)

    def close(step, i):
        rows = pl.multiple_of((step * PER + i) * TOK, TOK)
        upper, lower = acc[pl.ds(rows, HD)], acc[pl.ds(rows + HD, HD)]
        opack[step, i] = jnp.where(
            low_64, swap(upper) / upper, lower / swap(lower)
        ).astype(bf16)

    def finish(n, _):
        group = NZ // 2 - 1 - n
        rest(group)
        for step in (2 * group + 1, 2 * group):
            for i in range(PER):
                close(step, i)
                o_copy(step, i).start()
        return 0

    lax.fori_loop(0, NZ // 2 - 1, finish, 0)
    rest(0)
    for i in range(PER):
        close(1, i)
        o_copy(1, i).start()
    for t in range(1, PER):
        close(0, other(t))
        o_copy(0, other(t)).start()
    close(0, mine)
    own_o = pltpu.make_async_copy(opack.at[0, mine], o_recv.at[me], own_sem.at[3])
    own_o.start()

    for t in range(1, PER):
        q_copy(0, other(t), mine).wait_send()
        kv_copy(0, other(t), mine).wait_send()
        o_copy(0, other(t)).wait_send()

    def sent(step, _):
        for i in range(PER):
            q_copy(step, i, mine).wait_send()
            kv_copy(step, i, mine).wait_send()
            o_copy(step, i).wait_send()
        return 0

    lax.fori_loop(1, NZ, sent, 0)

    def arrived(t, _):
        head = (me + t) % SEQ
        pltpu.make_async_remote_copy(
            opack.at[0, 0], o_recv.at[head], o_ss.at[0, 0], o_rs.at[head],
            device_id=dev(head), device_id_type=MESH,
        ).wait_recv()
        return 0

    lax.fori_loop(1, SEQ, arrived, 0)

    def moved(n, _):
        move_copy(n).wait()
        return 0

    lax.fori_loop(0, NZ, moved, 0)
    stay_copy.wait()
    own_o.wait()


PARTS = 4


def unpack_kernel(glen, heads, stay, incoming, giant_out, short_out, held, made, both, sems):
    moves = [
        pltpu.make_async_copy(ref, both.at[n], sems.at[n]) for n, ref in enumerate((stay, incoming))
    ]
    ends = [
        pltpu.make_async_copy(both.at[n], short_out.at[0, 0, n], sems.at[2 + 2 * PARTS + n])
        for n in range(2)
    ]
    per = HEADS // PARTS
    wide = FEAT // PARTS
    into = [
        pltpu.make_async_copy(
            heads.at[pl.ds(n * per, per)], held.at[pl.ds(n * per, per)], sems.at[2 + n]
        )
        for n in range(PARTS)
    ]
    out = [
        pltpu.make_async_copy(
            made.at[:, pl.ds(n * wide, wide)], giant_out.at[0, :, pl.ds(n * wide, wide)],
            sems.at[2 + PARTS + n],
        )
        for n in range(PARTS)
    ]
    for copy in into[:1] + moves + into[1:]:
        copy.start()
    me = lax.axis_index("seq")
    group_len = glen[lax.axis_index("grp")]
    low = lanes(HD) < HD
    row = me * TOK + lax.broadcasted_iota(jnp.int32, (HD, LANES), 0)
    for n in range(PARTS):
        into[n].wait()
        for j in range(n * PAIRS // PARTS, (n + 1) * PAIRS // PARTS):
            even, odd = held[2 * j].astype(f32), held[2 * j + 1].astype(f32)
            upper = jnp.where(low, even, swap(odd))
            lower = jnp.where(low, swap(even), odd)
            at = pl.ds(j * LANES, LANES)
            made[pl.ds(0, HD), at] = jnp.where(row < group_len, upper, 0.0).astype(bf16)
            made[pl.ds(HD, HD), at] = jnp.where(row + HD < group_len, lower, 0.0).astype(bf16)
        out[n].start()
        if n < 2:
            moves[n].wait()
            ends[n].start()
    for copy in out + ends:
        copy.wait()


def per_device(table, giant_q, giant_k, giant_v, giant_len, short_q, short_k, short_v, short_len, short_move):
    any_spec = pl.BlockSpec(memory_space=pl.ANY)
    smem = pl.BlockSpec(memory_space=pltpu.SMEM)
    dma = pltpu.SemaphoreType.DMA
    heads, stay, incoming = pl.pallas_call(
        main_kernel,
        out_shape=(
            jax.ShapeDtypeStruct((HEADS, HD, LANES), bf16),
            jax.ShapeDtypeStruct((TOK, FEAT), bf16),
            jax.ShapeDtypeStruct((TOK, FEAT), bf16),
        ),
        in_specs=[smem] * 3 + [any_spec] * 7,
        out_specs=(any_spec,) * 3,
        scratch_shapes=[
            pltpu.VMEM((6, TOK, FEAT), bf16),
            pltpu.VMEM((2, TOK, LANES), f32),
            pltpu.VMEM((TOK, LANES), f32),
            pltpu.VMEM((TOK, LANES), f32),
            pltpu.VMEM((SEQ, HD, LANES), bf16),
            pltpu.VMEM((SEQ, TOK, LANES), bf16),
            pltpu.VMEM((NZ, PER, HD, LANES), bf16),
            pltpu.VMEM((NZ, CHUNK, LANES), bf16),
            pltpu.VMEM((NTOK, LANES), bf16),
            pltpu.VMEM((NTOK, LANES), f32),
            pltpu.VMEM((NTOK, LANES), f32),
            pltpu.VMEM(((NZ - EARLY) * CHUNK, LANES), bf16),
            pltpu.VMEM(((NZ - EARLY) * CHUNK, LANES), bf16),
            pltpu.VMEM((NZ, PER, HD, LANES), bf16),
            pltpu.VMEM((TOK, FEAT), bf16),
            pltpu.VMEM((TOK, FEAT), bf16),
            dma((6,)),
            dma((2,)),
            dma((4,)),
            dma((NZ, PER)),
            dma((NZ, PER)),
            dma((NZ, PER)),
            dma((NZ, PER)),
            dma((NZ, PER)),
            dma((SEQ,)),
            dma((NZ,)),
            dma((NZ,)),
        ],
        compiler_params=pltpu.CompilerParams(
            collective_id=0, has_side_effects=True, vmem_limit_bytes=56 << 20
        ),
    )(giant_len, short_len, short_move, table, giant_q, giant_k, giant_v, short_q, short_k, short_v)
    return pl.pallas_call(
        unpack_kernel,
        out_shape=(
            jax.ShapeDtypeStruct((1, TOK, FEAT), bf16),
            jax.ShapeDtypeStruct((1, 1, 2, TOK, FEAT), bf16),
        ),
        in_specs=[smem] + [any_spec] * 3,
        out_specs=(any_spec, any_spec),
        scratch_shapes=[
            pltpu.VMEM((HEADS, HD, LANES), bf16),
            pltpu.VMEM((TOK, FEAT), bf16),
            pltpu.VMEM((2, TOK, FEAT), bf16),
            dma((4 + 2 * PARTS,)),
        ],
        compiler_params=pltpu.CompilerParams(vmem_limit_bytes=56 << 20),
    )(giant_len, heads, stay, incoming)


def solution(mesh):
    table = angle_table()
    in_specs = (
        P(),
        P("grp", "seq", None),
        P("grp", "seq", None),
        P("grp", "seq", None),
        P(),
        P("grp", "seq", None, None),
        P("grp", "seq", None, None),
        P("grp", "seq", None, None),
        P(),
        P(),
    )
    out_specs = (P("grp", "seq", None), P("grp", "seq", None, None, None))
    body = jax.shard_map(
        per_device, mesh=mesh, in_specs=in_specs, out_specs=out_specs, check_vma=False
    )

    def run(*arrays):
        return body(jnp.asarray(table), *arrays)

    return run
```
